32 devices in a mesh: replica: 16 (over z, y, x), tensor: 2 (over core).
Axes of the slice: x: 2, y: 2, z: 4, core: 2. Of those that a mesh axis runs over, the one named last changes fastest.
Arguments:
- tokens: bfloat16 [8192, 8192], P(('replica', 'tensor')), may hold values from -6 to 6
- norm_gain: bfloat16 [8192], replicated, may hold values from 0.099609375 to 1.8984375
- key_weight: bfloat16 [16, 8192, 1024], P('replica', None, 'tensor'), may hold values from -0.0625 to 0.0625
- inner_params: bfloat16 [16, 2, 1024, 512], P('replica', 'tensor'), may hold values from -6 to 6
- outer_params: float32 [2, 1024, 512], P('tensor', 'replica'), may hold values from -6 to 6
- outer_momentum: float32 [2, 1024, 512], P('tensor', 'replica'), may hold values from -3 to 3
Outputs:
- key_rows: bfloat16 [8192, 1024], P('replica', 'tensor')
- new_outer: float32 [2, 1024, 512], P('tensor', 'replica')
- new_momentum: float32 [2, 1024, 512], P('tensor', 'replica')
- synced_params: bfloat16 [2, 1024, 512], P('tensor')
The draws below stay inside these ranges and needn't reach their ends.
All inputs are finite; a program needn't handle non-finite values.
Results may differ from the reference program's by a relative error of at most 0.0049.
Values may be sent and summed in bfloat16 or wider, within the bound.
A program may use at most 64 MiB of HBM per device.

```python
import math
import jax
import jax.numpy as jnp
from jax import lax

D = 8192
KVH = 8
HD = 128
TOK = 512
FRAG_ROWS = 1024
FRAG_COLS = 512
TOKENS = 8192
N_REPLICA = 16
N_TENSOR = 2


def strengthened(array, rng, source, target, shards_of, factor):
    def block_of(dim):
        return (jnp.arange(array.shape[dim]) // (array.shape[dim] // shards_of)).reshape((-1,) + (1,) * (array.ndim - 1 - dim))

    first = jax.random.permutation(rng, shards_of)[block_of(target)]
    other_side = (block_of(target) + shards_of // 2) % shards_of
    return jnp.where((block_of(source) == first) | (block_of(source) == other_side), factor * array, array)


def steps_of(own_key, shape, pieces, low, largest):
    gain = 1.0
    for axis_at, parts in pieces:
        heights = jax.random.uniform(jax.random.fold_in(jax.random.fold_in(own_key, 6), axis_at), (parts,), jnp.float32, low / len(pieces), largest / len(pieces))
        gain = gain * jnp.repeat(jnp.exp(heights), shape[axis_at] // parts).reshape((-1,) + (1,) * (len(shape) - 1 - axis_at))
    return gain


def centred(key, shape, width, limit, pieces=(), held_as=jnp.bfloat16):
    loudness = steps_of(key, shape, pieces, -0.22, 0.18) if pieces else 1.0
    result = jax.random.normal(key, shape, jnp.float32) * width * loudness
    return jnp.minimum(jnp.maximum(result, -limit), limit).astype(held_as)


def gaussian_with(key, extent, spread, limit, cuts, heavy, kind=jnp.bfloat16):
    entries = spread * jax.random.normal(key, extent, jnp.float32)
    if cuts:
        entries = entries * steps_of(key, extent, cuts, -0.22, 0.18)
    return jnp.clip(strengthened(entries, jax.random.fold_in(key, 3), *heavy), -limit, limit).astype(kind)


def setup_inputs(seed: int = 0) -> dict:
    key_of = jax.random.split(jax.random.key(seed), 7)
    return {
        "tokens": centred(key_of[0], (TOKENS, D), 1.0, 6.0, ((0, 32),)),
        "norm_gain": jnp.clip(1.0 + 0.18 * jax.random.normal(key_of[1], (D,), jnp.float32), 0.099609375, 1.8984375).astype(jnp.bfloat16),
        "key_weight": centred(key_of[2], (N_REPLICA, D, KVH * HD), D ** -0.5, 0.0625, ((0, 16), (2, 2))),
        "inner_params": gaussian_with(key_of[3], (N_REPLICA, N_TENSOR, FRAG_ROWS, FRAG_COLS), 1.0, 6.0, ((0, 16), (1, 2)), (0, 2, 16, 2.0)),
        "outer_params": centred(key_of[4], (N_TENSOR, FRAG_ROWS, FRAG_COLS), 1.0, 6.0, ((0, 2), (1, 16)), jnp.float32),
        "outer_momentum": centred(key_of[5], (N_TENSOR, FRAG_ROWS, FRAG_COLS), 0.5, 3.0, ((0, 2), (1, 16)), jnp.float32),
    }


EPSILON = 1e-05
ROPE_BASE = 500000.0
LR_OUTER = 0.7
MOMENTUM_OUTER = 0.9

def rotate(keys_f32, positions):
    rows = keys_f32.shape[0]
    cols = keys_f32.shape[1]
    half = HD // 2
    shaped = keys_f32.reshape(rows, cols // HD, HD)
    index = jnp.arange(half).astype(jnp.float32)
    inverse = jnp.exp(-(2.0 * index / HD) * math.log(ROPE_BASE))
    angles = positions[:, None] * inverse[None, :]
    cosine = jnp.cos(angles)[:, None, :]
    sine = jnp.sin(angles)[:, None, :]
    first = shaped[:, :, :half]
    second = shaped[:, :, half:]
    joined = jnp.concatenate([first * cosine - second * sine, second * cosine + first * sine], axis=-1)
    return joined.reshape(rows, cols)

def reference(tokens, norm_gain, key_weight, inner_params, outer_params, outer_momentum):
    gain_f32 = norm_gain.astype(jnp.float32)
    positions = jnp.arange(TOK).astype(jnp.float32)

    def forward_one(pair):
        block, weight = pair
        block_f32 = block.astype(jnp.float32)
        scale = lax.rsqrt(lax.optimization_barrier(jnp.mean(block_f32 * block_f32, axis=-1, keepdims=True)) + EPSILON)
        normed = (block_f32 * scale * gain_f32).astype(jnp.bfloat16)
        projected = jnp.dot(normed, weight, preferred_element_type=jnp.float32)
        return rotate(projected, positions).astype(jnp.bfloat16)
    blocks = tokens.reshape(N_REPLICA, TOK, D)
    key_rows = lax.map(forward_one, (blocks, key_weight)).reshape(N_REPLICA * TOK, KVH * HD)
    summed = lax.optimization_barrier(jnp.sum(inner_params, axis=0, dtype=jnp.float32))
    delta = outer_params - summed / N_REPLICA
    new_momentum = MOMENTUM_OUTER * outer_momentum + delta
    new_outer = outer_params - LR_OUTER * (delta + MOMENTUM_OUTER * new_momentum)
    synced_params = new_outer.astype(jnp.bfloat16)
    return (key_rows, new_outer, new_momentum, synced_params)
```

```python
import functools
import math

import jax
import jax.numpy as jnp
import numpy as np
from jax import lax
from jax.experimental import pallas as pl
from jax.experimental.pallas import tpu as pltpu
from jax.sharding import PartitionSpec as P

HD = 128
EPSILON = 1e-05
ROPE_BASE = 500000.0
LR_OUTER = 0.7
MOMENTUM_OUTER = 0.9

MESH = pl.DeviceIdType.MESH
F32 = jnp.float32
BF16 = jnp.bfloat16

NORM_ROWS = 32
NORM_COLS = 512
K_STEP = 1024


def rotary_tables(rows):
    half = HD // 2
    index = np.arange(half, dtype=np.float32)
    inverse = np.exp(-(2.0 * index / HD) * math.log(ROPE_BASE)).astype(np.float32)
    angles = (np.arange(rows, dtype=np.float32)[:, None] * inverse[None, :]).astype(np.float64)
    cosine, sine = np.cos(angles), np.sin(angles)
    return np.stack(
        [np.concatenate([cosine, cosine], 1), np.concatenate([-sine, sine], 1)]
    ).astype(np.float32)


def kernel(
    sizes,
    tokens, gain, weight, inner, outer, moment, tables,
    keys_out, outer_out, moment_out, synced,
    tok_v, gain_v, w_v, inner_v, outer_v, moment_v, tables_v, normed_v, acc_v, keys_v,
    rs1a, rs1b, part1a, part1b, keepa, keepb, rs2a, rs2b, part2, own, rs3, piece_v,
    load_sem, tok_sem, w_sem, store_sem,
    s1_send, s1_recv, s2_send, s2_recv, s3_send, s3_recv,
    gz_send, gz_recv, gx_send, gx_recv, gy_send, gy_recv, dx_send, dx_recv, dy_send, dy_recv,
    n_send, n_recv,
):
    Z, T, tr, D, nc, rp, FC, nch, nw = sizes
    H = FC // 2
    R = Z * 4
    rep = lax.axis_index("replica")
    me_t = lax.axis_index("tensor")
    z, y, x = rep // 4, lax.rem(rep // 2, 2), lax.rem(rep, 2)
    oy, ox = 1 - y, 1 - x
    x_peer = (z * 4 + y * 2 + ox, me_t)
    y_peer = (z * 4 + oy * 2 + x, me_t)
    offsets = sorted(range(1, Z), key=lambda o: (-min(o, Z - o), o)) + [0]
    last = Z - 1

    def z_at(o):
        return lax.rem(z + o, Z)

    def z_peer(o):
        return (z_at(o) * 4 + y * 2 + x, me_t)

    rows_per = tr // nch
    k_per = D // nw
    load_inner = pltpu.make_async_copy(inner, inner_v, load_sem.at[0])
    load_gain = pltpu.make_async_copy(gain, gain_v, load_sem.at[1])
    load_outer = pltpu.make_async_copy(outer, outer_v, load_sem.at[2])
    load_moment = pltpu.make_async_copy(moment, moment_v, load_sem.at[3])
    load_tables = pltpu.make_async_copy(tables, tables_v, load_sem.at[4])
    load_tok = [
        pltpu.make_async_copy(
            tokens.at[pl.ds(c * rows_per, rows_per)],
            tok_v.at[pl.ds(c * rows_per, rows_per)],
            tok_sem.at[c],
        )
        for c in range(nch)
    ]
    load_w = [
        pltpu.make_async_copy(
            weight.at[0, pl.ds(c * k_per, k_per)], w_v.at[pl.ds(c * k_per, k_per)], w_sem.at[c]
        )
        for c in range(nw)
    ]
    load_gain.start()
    load_tok[0].start()
    load_inner.start()
    for c in range(1, nch):
        load_tok[c].start()
    for c in range(nw):
        load_w[c].start()
    load_outer.start()
    load_moment.start()
    load_tables.start()

    barrier = pltpu.get_barrier_semaphore()
    partners = [x_peer, y_peer]
    partners += [z_peer(o) for o in range(1, Z)]
    partners += [(rep, lax.rem(me_t + k, T)) for k in range(1, T)]
    for partner in partners:
        pl.semaphore_signal(barrier, inc=1, device_id=partner, device_id_type=MESH)
    pl.semaphore_wait(barrier, len(partners))

    sent = []

    def remote(src, dst, send_sem, recv_sem, device):
        return pltpu.make_async_remote_copy(
            src_ref=src, dst_ref=dst, send_sem=send_sem, recv_sem=recv_sem,
            device_id=device, device_id_type=MESH,
        )

    def start(copy):
        copy.start()
        sent.append(copy)
        return copy

    first_a, first_b = [], []
    for d, o in enumerate(offsets):
        zc = z_at(o)
        first_a.append(start(remote(
            inner.at[zc, :, ox, :, pl.ds(0, H)], rs1a.at[d],
            s1_send.at[2 * d], s1_recv.at[2 * d], x_peer)))
        first_b.append(start(remote(
            inner.at[zc, oy, :, :, pl.ds(H, H)], rs1b.at[d],
            s1_send.at[2 * d + 1], s1_recv.at[2 * d + 1], y_peer)))

    def norm_copy(k, c, source, device):
        rows = pl.ds(c * rows_per, rows_per)
        i = (k - 1) * nch + c
        return remote(
            normed_v.at[source, rows], normed_v.at[source, rows], n_send.at[i], n_recv.at[i], device
        )

    def norm(c):
        if c == 0:
            load_gain.wait()
        load_tok[c].wait()

        def block(i, carry):
            rows = pl.ds(pl.multiple_of(c * rows_per + i * NORM_ROWS, NORM_ROWS), NORM_ROWS)
            total = jnp.zeros((NORM_ROWS, 128), F32)
            for j in range(0, D, 128):
                v = tok_v[rows, pl.ds(j, 128)].astype(F32)
                total = total + v * v
            scale = lax.rsqrt(jnp.sum(total, axis=-1, keepdims=True) / D + EPSILON)
            for j in range(0, D, NORM_COLS):
                cols = pl.ds(j, NORM_COLS)
                v = tok_v[rows, cols].astype(F32)
                normed_v[me_t, rows, cols] = (v * scale * gain_v[:, cols].astype(F32)).astype(BF16)
            return carry

        lax.fori_loop(0, rows_per // NORM_ROWS, block, 0)
        for k in range(1, T):
            start(norm_copy(k, c, me_t, (rep, lax.rem(me_t + k, T))))

    second_a, second_b, third = [None] * Z, [None] * Z, [None] * Z

    def step_a(d):
        zc = z_at(offsets[d])
        if d == 0:
            load_inner.wait()
        first_a[d].wait_recv()
        part1a[d] = (inner_v[zc, oy, x, :, :H].astype(F32) + rs1a[d, oy].astype(F32)).astype(BF16)
        second_a[d] = start(remote(
            part1a.at[d], rs2a.at[d], s2_send.at[2 * d], s2_recv.at[2 * d], y_peer))
        keepa[d] = inner_v[zc, y, x, :, :H].astype(F32) + rs1a[d, y].astype(F32)
        first_b[d].wait_recv()
        part1b[d] = (inner_v[zc, y, ox, :, H:].astype(F32) + rs1b[d, ox].astype(F32)).astype(BF16)
        second_b[d] = start(remote(
            part1b.at[d], rs2b.at[d], s2_send.at[2 * d + 1], s2_recv.at[2 * d + 1], x_peer))
        keepb[d] = inner_v[zc, y, x, :, H:].astype(F32) + rs1b[d, x].astype(F32)

    def step_b(d):
        second_a[d].wait_recv()
        second_b[d].wait_recv()
        suma = keepa[d] + rs2a[d].astype(F32)
        sumb = keepb[d] + rs2b[d].astype(F32)
        if d == last:
            own[:, :H] = suma
            own[:, H:] = sumb
        else:
            part2[d, :, :H] = suma.astype(BF16)
            part2[d, :, H:] = sumb.astype(BF16)
            third[d] = start(remote(
                part2.at[d], rs3.at[d], s3_send.at[d], s3_recv.at[d], z_peer(offsets[d])))

    stores = []

    def store(src, dst, i):
        copy = pltpu.make_async_copy(src, dst, store_sem.at[i])
        copy.start()
        stores.append(copy)

    here = synced.at[z, y, x]
    gather_z, gather_x, gather_y, diag_x, diag_y = ([None] * Z for _ in range(5))

    def spread(d, src):
        zp = lax.rem(z + Z - offsets[d], Z)
        dst = synced.at[zp, y, x]
        gather_y[d] = start(remote(src, dst, gy_send.at[d], gy_recv.at[d], y_peer))
        gather_x[d] = start(remote(src, dst, gx_send.at[d], gx_recv.at[d], x_peer))

    def step_c():
        load_outer.wait()
        load_moment.wait()
        summed = own[...]
        for d in range(last):
            third[d].wait_recv()
            summed = summed + rs3[d].astype(F32)
        outer_rows = outer_v[0]
        delta = outer_rows - summed / R
        moment_next = MOMENTUM_OUTER * moment_v[0] + delta
        outer_next = outer_rows - LR_OUTER * (delta + MOMENTUM_OUTER * moment_next)
        piece_v[...] = outer_next.astype(BF16)
        for d in range(last):
            gather_z[d] = start(remote(
                piece_v, here, gz_send.at[d], gz_recv.at[d], z_peer(offsets[d])))
        spread(last, piece_v)
        outer_v[0] = outer_next
        moment_v[0] = moment_next
        store(outer_v, outer_out, 0)
        store(moment_v, moment_out, 1)
        store(piece_v, here, 2)

    def step_z(d):
        zp = lax.rem(z + Z - offsets[d], Z)
        gather_z[d].wait_recv()
        spread(d, synced.at[zp, y, x])

    def step_f(d):
        zp = lax.rem(z + Z - offsets[d], Z)
        gather_y[d].wait_recv()
        from_y = synced.at[zp, oy, x, :, pl.ds(0, H)]
        diag_x[d] = start(remote(from_y, from_y, dx_send.at[d], dx_recv.at[d], x_peer))
        gather_x[d].wait_recv()
        from_x = synced.at[zp, y, ox, :, pl.ds(H, H)]
        diag_y[d] = start(remote(from_x, from_x, dy_send.at[d], dy_recv.at[d], y_peer))

    def project(k, part):
        slot = lax.rem(me_t + T - k, T)
        if k == 0:
            load_w[part].wait()
        elif part == 0:
            for c in range(nch):
                norm_copy(k, c, slot, (rep, lax.rem(me_t + k, T))).wait_recv()

        def block(i, carry):
            depth = pl.ds(pl.multiple_of(part * k_per + i * K_STEP, K_STEP), K_STEP)
            acc_v[...] += jnp.dot(
                normed_v[slot, :, depth], w_v[depth, :], preferred_element_type=F32
            )
            return carry

        if part == 0:
            acc_v[...] = jnp.zeros_like(acc_v)
        lax.fori_loop(0, k_per // K_STEP, block, 0)

    def turn(k):
        slot = lax.rem(me_t + T - k, T)
        if k == 0:
            load_tables.wait()
        rows = pl.ds(pl.multiple_of(slot * tr, tr), tr)
        cosine = tables_v[0, rows]
        sine = tables_v[1, rows]
        for h in range(nc // HD):
            cols = pl.ds(h * HD, HD)
            v = acc_v[:, cols]
            keys_v[rows, cols] = (v * cosine + pltpu.roll(v, HD // 2, 1) * sine).astype(BF16)
        store(keys_v.at[rows], keys_out.at[rows], 3 + k)

    compute = [functools.partial(norm, c) for c in range(nch)]
    for k in range(T):
        compute += [functools.partial(project, k, part) for part in range(nw)]
        compute.append(functools.partial(turn, k))
    compute = compute[::-1]

    def work(count=1):
        for _ in range(count):
            if compute:
                compute.pop()()

    work(1)
    for d in range(Z):
        work(1)
        step_a(d)
        if d >= 1:
            step_b(d - 1)
    work(1)
    step_b(last)
    work(max(3, len(compute) - 5))
    step_c()
    work(1)
    step_f(last)
    for d in range(last):
        work(1)
        step_z(d)
        if d >= 1:
            step_f(d - 1)
    work(len(compute))
    step_f(last - 1)
    for d in range(Z):
        diag_x[d].wait_recv()
        diag_y[d].wait_recv()
    for copy in sent:
        copy.wait_send()
    for copy in stores:
        copy.wait()


def solution(mesh):
    R, T = mesh.shape["replica"], mesh.shape["tensor"]
    Z = R // 4

    def body(tokens, norm_gain, key_weight, inner_params, outer_params, outer_momentum):
        tr, D = tokens.shape
        nc = key_weight.shape[2]
        rows, FC = inner_params.shape[2:]
        rp = rows // R
        H = FC // 2
        tok = tr * T
        nch = max(1, tr // 64)
        nw = 4
        inner = inner_params.reshape(Z, 2, 2, rp, FC)
        gain = norm_gain.reshape(1, D)
        tables = jnp.asarray(rotary_tables(tok))
        sizes = (Z, T, tr, D, nc, rp, FC, nch, nw)
        vm = pltpu.VMEM
        dma = lambda n: pltpu.SemaphoreType.DMA((n,))
        scratch = [
            vm((tr, D), BF16), vm((1, D), BF16), vm((D, nc), BF16),
            vm((Z, 2, 2, rp, FC), BF16), vm((1, rp, FC), F32), vm((1, rp, FC), F32),
            vm((2, tok, HD), F32), vm((T, tr, D), BF16), vm((tr, nc), F32), vm((tok, nc), BF16),
            vm((Z, 2, rp, H), BF16), vm((Z, 2, rp, H), BF16),
            vm((Z, rp, H), BF16), vm((Z, rp, H), BF16),
            vm((Z, rp, H), F32), vm((Z, rp, H), F32),
            vm((Z, rp, H), BF16), vm((Z, rp, H), BF16),
            vm((Z, rp, FC), BF16), vm((rp, FC), F32), vm((Z, rp, FC), BF16), vm((rp, FC), BF16),
            dma(5), dma(nch), dma(nw), dma(3 + T),
            dma(2 * Z), dma(2 * Z), dma(2 * Z), dma(2 * Z), dma(Z), dma(Z),
            dma(Z), dma(Z), dma(Z), dma(Z), dma(Z), dma(Z), dma(Z), dma(Z), dma(Z), dma(Z),
            dma(nch * (T - 1)), dma(nch * (T - 1)),
        ]
        anywhere = pl.BlockSpec(memory_space=pl.ANY)
        keys, outer_next, moment_next, synced = pl.pallas_call(
            functools.partial(kernel, sizes),
            out_shape=(
                jax.ShapeDtypeStruct((tok, nc), BF16),
                jax.ShapeDtypeStruct((1, rp, FC), F32),
                jax.ShapeDtypeStruct((1, rp, FC), F32),
                jax.ShapeDtypeStruct((Z, 2, 2, rp, FC), BF16),
            ),
            in_specs=[anywhere] * 7,
            out_specs=(anywhere,) * 4,
            scratch_shapes=scratch,
            compiler_params=pltpu.CompilerParams(
                collective_id=0, has_side_effects=True, vmem_limit_bytes=48 * 2**20
            ),
            name="outer_step_and_keys",
        )(tokens, gain, key_weight, inner, outer_params, outer_momentum, tables)
        return keys, outer_next, moment_next, synced.reshape(1, rows, FC)

    in_specs = (
        P(("replica", "tensor"), None),
        P(),
        P("replica", None, "tensor"),
        P("replica", "tensor", None, None),
        P("tensor", "replica", None),
        P("tensor", "replica", None),
    )
    out_specs = (
        P("replica", "tensor"),
        P("tensor", "replica", None),
        P("tensor", "replica", None),
        P("tensor", None, None),
    )
    return jax.shard_map(body, mesh=mesh, in_specs=in_specs, out_specs=out_specs, check_vma=False)
```

```python
import functools
import math

import jax
import jax.numpy as jnp
import numpy as np
from jax import lax
from jax.experimental import pallas as pl
from jax.experimental.pallas import tpu as pltpu
from jax.sharding import PartitionSpec as P

HD = 128
EPSILON = 1e-05
ROPE_BASE = 500000.0
LR_OUTER = 0.7
MOMENTUM_OUTER = 0.9

MESH = pl.DeviceIdType.MESH
F32 = jnp.float32
BF16 = jnp.bfloat16

NORM_ROWS = 32
NORM_COLS = 512
K_STEP = 1024
VMEM_GRANT = 64 * 2**20 - 2**16


def rotary_tables(rows):
    half = HD // 2
    index = np.arange(half, dtype=np.float32)
    inverse = np.exp(-(2.0 * index / HD) * math.log(ROPE_BASE)).astype(np.float32)
    angles = (np.arange(rows, dtype=np.float32)[:, None] * inverse[None, :]).astype(np.float64)
    cosine, sine = np.cos(angles), np.sin(angles)
    return np.stack(
        [np.concatenate([cosine, cosine], 1), np.concatenate([-sine, sine], 1)]
    ).astype(np.float32)


def kernel(
    sizes,
    tokens, gain, weight, inner, outer, moment, tables,
    keys_out, outer_out, moment_out, synced,
    tok_v, gain_v, w_v, inner_v, outer_v, moment_v, tables_v, normed_v, acc_v, keys_v,
    rs1, part1, keep, rs2, part2, own, rs3, piece_v,
    load_sem, tok_sem, w_sem, store_sem,
    s1_send, s1_recv, s2_send, s2_recv, s3_send, s3_recv,
    gz_send, gz_recv, gx_send, gx_recv, gy_send, gy_recv, diag_send, diag_recv,
    n_send, n_recv,
):
    Z, T, tr, D, nc, rp, FC, nch, nw = sizes
    R = Z * 4
    rep = lax.axis_index("replica")
    me_t = lax.axis_index("tensor")
    z, y, x = rep // 4, lax.rem(rep // 2, 2), lax.rem(rep, 2)
    oy, ox = 1 - y, 1 - x
    x_peer = (z * 4 + y * 2 + ox, me_t)
    y_peer = (z * 4 + oy * 2 + x, me_t)
    offsets = sorted(range(1, Z), key=lambda o: (-min(o, Z - o), o)) + [0]
    last = Z - 1

    def z_at(o):
        return lax.rem(z + o, Z)

    def z_peer(o):
        return (z_at(o) * 4 + y * 2 + x, me_t)

    rows_per = tr // nch
    k_per = D // nw
    load_inner = pltpu.make_async_copy(inner, inner_v, load_sem.at[0])
    load_gain = pltpu.make_async_copy(gain, gain_v, load_sem.at[1])
    load_outer = pltpu.make_async_copy(outer, outer_v, load_sem.at[2])
    load_moment = pltpu.make_async_copy(moment, moment_v, load_sem.at[3])
    load_tables = pltpu.make_async_copy(tables, tables_v, load_sem.at[4])
    load_tok = [
        pltpu.make_async_copy(
            tokens.at[pl.ds(c * rows_per, rows_per)],
            tok_v.at[pl.ds(c * rows_per, rows_per)],
            tok_sem.at[c],
        )
        for c in range(nch)
    ]
    load_w = [
        pltpu.make_async_copy(
            weight.at[0, pl.ds(c * k_per, k_per)], w_v.at[pl.ds(c * k_per, k_per)], w_sem.at[c]
        )
        for c in range(nw)
    ]
    load_gain.start()
    load_tok[0].start()
    load_inner.start()
    for c in range(1, nch):
        load_tok[c].start()
    for c in range(nw):
        load_w[c].start()
    load_outer.start()
    load_moment.start()
    load_tables.start()

    barrier = pltpu.get_barrier_semaphore()
    partners = [x_peer, y_peer]
    partners += [z_peer(o) for o in range(1, Z)]
    partners += [(rep, lax.rem(me_t + k, T)) for k in range(1, T)]
    for partner in partners:
        pl.semaphore_signal(barrier, inc=1, device_id=partner, device_id_type=MESH)
    pl.semaphore_wait(barrier, len(partners))

    sent = []

    def remote(src, dst, send_sem, recv_sem, device):
        return pltpu.make_async_remote_copy(
            src_ref=src, dst_ref=dst, send_sem=send_sem, recv_sem=recv_sem,
            device_id=device, device_id_type=MESH,
        )

    def start(copy):
        copy.start()
        sent.append(copy)
        return copy

    by_x = [o % 2 == 0 for o in offsets]
    first = []
    for d, o in enumerate(offsets):
        zc = z_at(o)
        src = inner.at[zc, :, ox] if by_x[d] else inner.at[zc, oy]
        first.append(start(remote(
            src, rs1.at[d], s1_send.at[d], s1_recv.at[d], x_peer if by_x[d] else y_peer)))

    def norm_copy(k, c, source, device):
        rows = pl.ds(c * rows_per, rows_per)
        i = (k - 1) * nch + c
        return remote(
            normed_v.at[source, rows], normed_v.at[source, rows], n_send.at[i], n_recv.at[i], device
        )

    def norm(c):
        if c == 0:
            load_gain.wait()
        load_tok[c].wait()

        def block(i, carry):
            rows = pl.ds(pl.multiple_of(c * rows_per + i * NORM_ROWS, NORM_ROWS), NORM_ROWS)
            total = jnp.zeros((NORM_ROWS, 128), F32)
            for j in range(0, D, 128):
                v = tok_v[rows, pl.ds(j, 128)].astype(F32)
                total = total + v * v
            scale = lax.rsqrt(jnp.sum(total, axis=-1, keepdims=True) / D + EPSILON)
            for j in range(0, D, NORM_COLS):
                cols = pl.ds(j, NORM_COLS)
                v = tok_v[rows, cols].astype(F32)
                normed_v[me_t, rows, cols] = (v * scale * gain_v[cols].astype(F32).reshape(1, NORM_COLS)).astype(BF16)
            return carry

        lax.fori_loop(0, rows_per // NORM_ROWS, block, 0)
        for k in range(1, T):
            start(norm_copy(k, c, me_t, (rep, lax.rem(me_t + k, T))))

    second, third = [None] * Z, [None] * Z

    def step_a(d):
        zc = z_at(offsets[d])
        if d == 0:
            load_inner.wait()
        first[d].wait_recv()
        if by_x[d]:
            mine, other, to, peer = y, inner_v[zc, oy, x], oy, y_peer
        else:
            mine, other, to, peer = x, inner_v[zc, y, ox], ox, x_peer
        part1[d] = (other.astype(F32) + rs1[d, to].astype(F32)).astype(BF16)
        second[d] = start(remote(part1.at[d], rs2.at[d], s2_send.at[d], s2_recv.at[d], peer))
        keep[d] = inner_v[zc, y, x].astype(F32) + rs1[d, mine].astype(F32)

    def step_b(d):
        second[d].wait_recv()
        total = keep[d] + rs2[d].astype(F32)
        if d == last:
            own[...] = total
        else:
            part2[d] = total.astype(BF16)
            third[d] = start(remote(
                part2.at[d], rs3.at[d], s3_send.at[d], s3_recv.at[d], z_peer(offsets[d])))

    stores = []

    def store(src, dst, i):
        copy = pltpu.make_async_copy(src, dst, store_sem.at[i])
        copy.start()
        stores.append(copy)

    here = synced.at[z, y, x]
    gather_z, gather_x, gather_y, diag = ([None] * Z for _ in range(4))

    def spread(d, src):
        zp = lax.rem(z + Z - offsets[d], Z)
        dst = synced.at[zp, y, x]
        gather_y[d] = start(remote(src, dst, gy_send.at[d], gy_recv.at[d], y_peer))
        gather_x[d] = start(remote(src, dst, gx_send.at[d], gx_recv.at[d], x_peer))

    def step_c():
        load_outer.wait()
        load_moment.wait()
        summed = own[...]
        for d in range(last):
            third[d].wait_recv()
            summed = summed + rs3[d].astype(F32)
        outer_rows = outer_v[0]
        delta = outer_rows - summed / R
        moment_next = MOMENTUM_OUTER * moment_v[0] + delta
        outer_next = outer_rows - LR_OUTER * (delta + MOMENTUM_OUTER * moment_next)
        piece_v[...] = outer_next.astype(BF16)
        for d in range(last):
            gather_z[d] = start(remote(
                piece_v, here, gz_send.at[d], gz_recv.at[d], z_peer(offsets[d])))
        spread(last, piece_v)
        outer_v[0] = outer_next
        moment_v[0] = moment_next
        store(outer_v, outer_out, 0)
        store(moment_v, moment_out, 1)
        store(piece_v, here, 2)

    def step_z(d):
        zp = lax.rem(z + Z - offsets[d], Z)
        gather_z[d].wait_recv()
        spread(d, synced.at[zp, y, x])

    def step_f(d):
        zp = lax.rem(z + Z - offsets[d], Z)
        if by_x[d]:
            gather_y[d].wait_recv()
            piece, peer = synced.at[zp, oy, x], x_peer
        else:
            gather_x[d].wait_recv()
            piece, peer = synced.at[zp, y, ox], y_peer
        diag[d] = start(remote(piece, piece, diag_send.at[d], diag_recv.at[d], peer))

    def project(k, part):
        slot = lax.rem(me_t + T - k, T)
        if k == 0:
            load_w[part].wait()
        elif part == 0:
            for c in range(nch):
                norm_copy(k, c, slot, (rep, lax.rem(me_t + k, T))).wait_recv()

        def block(i, carry):
            depth = pl.ds(pl.multiple_of(part * k_per + i * K_STEP, K_STEP), K_STEP)
            acc_v[...] += jnp.dot(
                normed_v[slot, :, depth], w_v[depth, :], preferred_element_type=F32
            )
            return carry

        if part == 0:
            acc_v[...] = jnp.zeros_like(acc_v)
        lax.fori_loop(0, k_per // K_STEP, block, 0)

    def turn(k):
        slot = lax.rem(me_t + T - k, T)
        if k == 0:
            load_tables.wait()
        rows = pl.ds(pl.multiple_of(slot * tr, tr), tr)
        cosine = tables_v[0, rows]
        sine = tables_v[1, rows]
        for h in range(nc // HD):
            cols = pl.ds(h * HD, HD)
            v = acc_v[:, cols]
            keys_v[rows, cols] = (v * cosine + pltpu.roll(v, HD // 2, 1) * sine).astype(BF16)
        store(keys_v.at[rows], keys_out.at[rows], 3 + k)

    compute = [functools.partial(norm, c) for c in range(nch)]
    for k in range(T):
        compute += [functools.partial(project, k, part) for part in range(nw)]
        compute.append(functools.partial(turn, k))
    compute = compute[::-1]

    def work(count=1):
        for _ in range(count):
            if compute:
                compute.pop()()

    work(1)
    for d in range(Z):
        work(1)
        step_a(d)
        if d >= 1:
            step_b(d - 1)
    step_b(last)
    work(nw + 1 - max(0, Z - nch) - (1 if Z < nch else 0))
    step_c()
    step_f(last)
    for d in range(last):
        step_z(d)
        work(1)
        step_f(d)
        work(1)
    work(len(compute))
    for d in range(Z):
        (gather_x if by_x[d] else gather_y)[d].wait_recv()
        diag[d].wait_recv()
    for copy in sent:
        copy.wait_send()
    for copy in stores:
        copy.wait()


def write_out(keys, outer, moment, synced, keys_out, outer_out, moment_out, synced_out, sem):
    pairs = ((synced, synced_out), (keys, keys_out), (outer, outer_out), (moment, moment_out))
    copies = [pltpu.make_async_copy(a, b, sem.at[i]) for i, (a, b) in enumerate(pairs)]
    for copy in copies:
        copy.start()
    for copy in copies:
        copy.wait()


def solution(mesh):
    R, T = mesh.shape["replica"], mesh.shape["tensor"]
    Z = R // 4

    def body(tokens, norm_gain, key_weight, inner_params, outer_params, outer_momentum):
        tr, D = tokens.shape
        nc = key_weight.shape[2]
        rows, FC = inner_params.shape[2:]
        rp = rows // R
        tok = tr * T
        nch = max(1, tr // 64)
        nw = 4
        inner = inner_params.reshape(Z, 2, 2, rp, FC)
        tables = jnp.asarray(rotary_tables(tok))
        sizes = (Z, T, tr, D, nc, rp, FC, nch, nw)
        vm = pltpu.VMEM
        dma = lambda n: pltpu.SemaphoreType.DMA((n,))
        scratch = [
            vm((tr, D), BF16), vm((D,), BF16), vm((D, nc), BF16),
            vm((Z, 2, 2, rp, FC), BF16), vm((1, rp, FC), F32), vm((1, rp, FC), F32),
            vm((2, tok, HD), F32), vm((T, tr, D), BF16), vm((tr, nc), F32), vm((tok, nc), BF16),
            vm((Z, 2, rp, FC), BF16), vm((Z, rp, FC), BF16), vm((Z, rp, FC), F32),
            vm((Z, rp, FC), BF16), vm((Z, rp, FC), BF16), vm((rp, FC), F32),
            vm((Z, rp, FC), BF16), vm((rp, FC), BF16),
            dma(5), dma(nch), dma(nw), dma(3 + T),
            dma(Z), dma(Z), dma(Z), dma(Z), dma(Z), dma(Z),
            dma(Z), dma(Z), dma(Z), dma(Z), dma(Z), dma(Z), dma(Z), dma(Z),
            dma(nch * (T - 1)), dma(nch * (T - 1)),
        ]
        anywhere = pl.BlockSpec(memory_space=pl.ANY)
        keys, outer_next, moment_next, synced = pl.pallas_call(
            functools.partial(kernel, sizes),
            out_shape=(
                jax.ShapeDtypeStruct((tok, nc), BF16),
                jax.ShapeDtypeStruct((1, rp, FC), F32),
                jax.ShapeDtypeStruct((1, rp, FC), F32),
                jax.ShapeDtypeStruct((Z, 2, 2, rp, FC), BF16),
            ),
            in_specs=[anywhere] * 7,
            out_specs=(anywhere,) * 4,
            scratch_shapes=scratch,
            compiler_params=pltpu.CompilerParams(
                collective_id=0, has_side_effects=True, vmem_limit_bytes=VMEM_GRANT
            ),
            name="outer_step_and_keys",
        )(tokens, norm_gain, key_weight, inner, outer_params, outer_momentum, tables)
        return pl.pallas_call(
            write_out,
            out_shape=(
                jax.ShapeDtypeStruct((tok, nc), BF16),
                jax.ShapeDtypeStruct((1, rp, FC), F32),
                jax.ShapeDtypeStruct((1, rp, FC), F32),
                jax.ShapeDtypeStruct((1, rows, FC), BF16),
            ),
            in_specs=[anywhere] * 4,
            out_specs=(pl.BlockSpec(memory_space=pltpu.HBM),) * 4,
            scratch_shapes=[dma(4)],
            compiler_params=pltpu.CompilerParams(vmem_limit_bytes=VMEM_GRANT),
            name="write_out",
        )(keys, outer_next, moment_next, synced.reshape(1, rows, FC))

    in_specs = (
        P(("replica", "tensor"), None),
        P(),
        P("replica", None, "tensor"),
        P("replica", "tensor", None, None),
        P("tensor", "replica", None),
        P("tensor", "replica", None),
    )
    out_specs = (
        P("replica", "tensor"),
        P("tensor", "replica", None),
        P("tensor", "replica", None),
        P("tensor", None, None),
    )
    return jax.shard_map(body, mesh=mesh, in_specs=in_specs, out_specs=out_specs, check_vma=False)
```

```python
import functools
import math

import jax
import jax.numpy as jnp
import numpy as np
from jax import lax
from jax.experimental import pallas as pl
from jax.experimental.pallas import tpu as pltpu
from jax.sharding import PartitionSpec as P

HD = 128
EPSILON = 1e-05
ROPE_BASE = 500000.0
LR_OUTER = 0.7
MOMENTUM_OUTER = 0.9

MESH = pl.DeviceIdType.MESH
F32 = jnp.float32
BF16 = jnp.bfloat16

NORM_ROWS = 32
NORM_COLS = 512
K_STEP = 1024
VMEM_GRANT = 48 * 2**20


def rotary_tables(rows):
    half = HD // 2
    index = np.arange(half, dtype=np.float32)
    inverse = np.exp(-(2.0 * index / HD) * math.log(ROPE_BASE)).astype(np.float32)
    angles = (np.arange(rows, dtype=np.float32)[:, None] * inverse[None, :]).astype(np.float64)
    cosine, sine = np.cos(angles), np.sin(angles)
    return np.stack(
        [np.concatenate([cosine, cosine], 1), np.concatenate([-sine, sine], 1)]
    ).astype(np.float32)


def kernel(
    sizes,
    tokens, gain, weight, inner, outer, moment, tables,
    keys_out, outer_out, moment_out, synced,
    tok_v, gain_v, w_v, inner_v, outer_v, moment_v, tables_v, normed_v, acc_v, keys_v,
    rs1, part1, keep, rs2, part2, own, rs3, piece_v,
    load_sem, tok_sem, w_sem, store_sem,
    s1_send, s1_recv, s2_send, s2_recv, s3_send, s3_recv,
    gz_send, gz_recv, gx_send, gx_recv, gy_send, gy_recv, diag_send, diag_recv,
    n_send, n_recv,
):
    Z, T, tr, D, nc, rp, FC, nch, nw = sizes
    R = Z * 4
    rep = lax.axis_index("replica")
    me_t = lax.axis_index("tensor")
    z, y, x = rep // 4, lax.rem(rep // 2, 2), lax.rem(rep, 2)
    oy, ox = 1 - y, 1 - x
    x_peer = (z * 4 + y * 2 + ox, me_t)
    y_peer = (z * 4 + oy * 2 + x, me_t)
    offsets = sorted(range(1, Z), key=lambda o: (-min(o, Z - o), o)) + [0]
    last = Z - 1

    def z_at(o):
        return lax.rem(z + o, Z)

    def z_peer(o):
        return (z_at(o) * 4 + y * 2 + x, me_t)

    rows_per = tr // nch
    k_per = D // nw
    load_inner = pltpu.make_async_copy(inner, inner_v, load_sem.at[0])
    load_gain = pltpu.make_async_copy(gain, gain_v, load_sem.at[1])
    load_outer = pltpu.make_async_copy(outer, outer_v, load_sem.at[2])
    load_moment = pltpu.make_async_copy(moment, moment_v, load_sem.at[3])
    load_tables = pltpu.make_async_copy(tables, tables_v, load_sem.at[4])
    load_tok = [
        pltpu.make_async_copy(
            tokens.at[pl.ds(c * rows_per, rows_per)],
            tok_v.at[pl.ds(c * rows_per, rows_per)],
            tok_sem.at[c],
        )
        for c in range(nch)
    ]
    load_w = [
        pltpu.make_async_copy(
            weight.at[0, pl.ds(c * k_per, k_per)], w_v.at[pl.ds(c * k_per, k_per)], w_sem.at[c]
        )
        for c in range(nw)
    ]
    load_inner.start()
    load_gain.start()
    load_tok[0].start()
    for c in range(1, nch):
        load_tok[c].start()
    for c in range(nw):
        load_w[c].start()
    load_outer.start()
    load_moment.start()
    load_tables.start()

    barrier = pltpu.get_barrier_semaphore()
    partners = [x_peer, y_peer]
    partners += [z_peer(o) for o in range(1, Z)]
    partners += [(rep, lax.rem(me_t + k, T)) for k in range(1, T)]
    for partner in partners:
        pl.semaphore_signal(barrier, inc=1, device_id=partner, device_id_type=MESH)
    pl.semaphore_wait(barrier, len(partners))

    sent = []

    def remote(src, dst, send_sem, recv_sem, device):
        return pltpu.make_async_remote_copy(
            src_ref=src, dst_ref=dst, send_sem=send_sem, recv_sem=recv_sem,
            device_id=device, device_id_type=MESH,
        )

    def start(copy):
        copy.start()
        sent.append(copy)
        return copy

    by_x = [o % 2 == 0 for o in offsets]
    first = []
    load_inner.wait()
    for d, o in enumerate(offsets):
        zc = z_at(o)
        src = inner_v.at[zc, :, ox] if by_x[d] else inner_v.at[zc, oy]
        first.append(start(remote(
            src, rs1.at[d], s1_send.at[d], s1_recv.at[d], x_peer if by_x[d] else y_peer)))

    def norm_copy(k, c, source, device):
        rows = pl.ds(c * rows_per, rows_per)
        i = (k - 1) * nch + c
        return remote(
            normed_v.at[source, rows], normed_v.at[source, rows], n_send.at[i], n_recv.at[i], device
        )

    def norm(c):
        if c == 0:
            load_gain.wait()
        load_tok[c].wait()

        def block(i, carry):
            rows = pl.ds(pl.multiple_of(c * rows_per + i * NORM_ROWS, NORM_ROWS), NORM_ROWS)
            total = jnp.zeros((NORM_ROWS, 128), F32)
            for j in range(0, D, 128):
                v = tok_v[rows, pl.ds(j, 128)].astype(F32)
                total = total + v * v
            scale = lax.rsqrt(jnp.sum(total, axis=-1, keepdims=True) / D + EPSILON)
            for j in range(0, D, NORM_COLS):
                cols = pl.ds(j, NORM_COLS)
                v = tok_v[rows, cols].astype(F32)
                normed_v[me_t, rows, cols] = (v * scale * gain_v[cols].astype(F32).reshape(1, NORM_COLS)).astype(BF16)
            return carry

        lax.fori_loop(0, rows_per // NORM_ROWS, block, 0)
        for k in range(1, T):
            start(norm_copy(k, c, me_t, (rep, lax.rem(me_t + k, T))))

    second, third = [None] * Z, [None] * Z

    def step_a(d):
        zc = z_at(offsets[d])
        first[d].wait_recv()
        if by_x[d]:
            mine, other, to, peer = y, inner_v[zc, oy, x], oy, y_peer
        else:
            mine, other, to, peer = x, inner_v[zc, y, ox], ox, x_peer
        part1[d] = (other.astype(F32) + rs1[d, to].astype(F32)).astype(BF16)
        second[d] = start(remote(part1.at[d], rs2.at[d], s2_send.at[d], s2_recv.at[d], peer))
        keep[d] = inner_v[zc, y, x].astype(F32) + rs1[d, mine].astype(F32)

    def step_b(d):
        second[d].wait_recv()
        total = keep[d] + rs2[d].astype(F32)
        if d == last:
            own[...] = total
        else:
            part2[d] = total.astype(BF16)
            third[d] = start(remote(
                part2.at[d], rs3.at[d], s3_send.at[d], s3_recv.at[d], z_peer(offsets[d])))

    stores = []

    def store(src, dst, i):
        copy = pltpu.make_async_copy(src, dst, store_sem.at[i])
        copy.start()
        stores.append(copy)

    here = synced.at[z, y, x]
    gather_z, gather_x, gather_y, diag = ([None] * Z for _ in range(4))

    def spread(d, src):
        zp = lax.rem(z + Z - offsets[d], Z)
        dst = synced.at[zp, y, x]
        gather_y[d] = start(remote(src, dst, gy_send.at[d], gy_recv.at[d], y_peer))
        gather_x[d] = start(remote(src, dst, gx_send.at[d], gx_recv.at[d], x_peer))

    def step_c():
        load_outer.wait()
        load_moment.wait()
        summed = own[...]
        for d in range(last):
            third[d].wait_recv()
            summed = summed + rs3[d].astype(F32)
        outer_rows = outer_v[0]
        delta = outer_rows - summed / R
        moment_next = MOMENTUM_OUTER * moment_v[0] + delta
        outer_next = outer_rows - LR_OUTER * (delta + MOMENTUM_OUTER * moment_next)
        piece_v[...] = outer_next.astype(BF16)
        for d in range(last):
            gather_z[d] = start(remote(
                piece_v, here, gz_send.at[d], gz_recv.at[d], z_peer(offsets[d])))
        spread(last, piece_v)
        outer_v[0] = outer_next
        moment_v[0] = moment_next
        store(outer_v, outer_out, 0)
        store(moment_v, moment_out, 1)
        store(piece_v, here, 2)

    def step_z(d):
        zp = lax.rem(z + Z - offsets[d], Z)
        gather_z[d].wait_recv()
        spread(d, synced.at[zp, y, x])

    def step_f(d):
        zp = lax.rem(z + Z - offsets[d], Z)
        if by_x[d]:
            gather_y[d].wait_recv()
            piece, peer = synced.at[zp, oy, x], x_peer
        else:
            gather_x[d].wait_recv()
            piece, peer = synced.at[zp, y, ox], y_peer
        diag[d] = start(remote(piece, piece, diag_send.at[d], diag_recv.at[d], peer))

    def project(k, part):
        slot = lax.rem(me_t + T - k, T)
        if k == 0:
            load_w[part].wait()
        elif part == 0:
            for c in range(nch):
                norm_copy(k, c, slot, (rep, lax.rem(me_t + k, T))).wait_recv()

        def block(i, carry):
            depth = pl.ds(pl.multiple_of(part * k_per + i * K_STEP, K_STEP), K_STEP)
            acc_v[...] += jnp.dot(
                normed_v[slot, :, depth], w_v[depth, :], preferred_element_type=F32
            )
            return carry

        if part == 0:
            acc_v[...] = jnp.zeros_like(acc_v)
        lax.fori_loop(0, k_per // K_STEP, block, 0)

    def turn(k):
        slot = lax.rem(me_t + T - k, T)
        if k == 0:
            load_tables.wait()
        rows = pl.ds(pl.multiple_of(slot * tr, tr), tr)
        cosine = tables_v[0, rows]
        sine = tables_v[1, rows]
        for h in range(nc // HD):
            cols = pl.ds(h * HD, HD)
            v = acc_v[:, cols]
            keys_v[rows, cols] = (v * cosine + pltpu.roll(v, HD // 2, 1) * sine).astype(BF16)
        store(keys_v.at[rows], keys_out.at[rows], 3 + k)

    compute = [functools.partial(norm, c) for c in range(nch)]
    for k in range(T):
        compute += [functools.partial(project, k, part) for part in range(nw)]
        compute.append(functools.partial(turn, k))
    compute = compute[::-1]

    def work(count=1):
        for _ in range(count):
            if compute:
                compute.pop()()

    work(1)
    for d in range(Z):
        work(1)
        step_a(d)
        if d >= 1:
            step_b(d - 1)
    step_b(last)
    work(nw + 1 - max(0, Z - nch) - (1 if Z < nch else 0))
    step_c()
    step_f(last)
    for d in range(last):
        step_z(d)
        work(1)
        step_f(d)
        work(1)
    work(len(compute))
    for d in range(Z):
        (gather_x if by_x[d] else gather_y)[d].wait_recv()
        diag[d].wait_recv()
    for copy in sent:
        copy.wait_send()
    for copy in stores:
        copy.wait()


def write_out(keys, outer, moment, synced, keys_out, outer_out, moment_out, synced_out, sem):
    pairs = ((synced, synced_out), (keys, keys_out), (outer, outer_out), (moment, moment_out))
    copies = [pltpu.make_async_copy(a, b, sem.at[i]) for i, (a, b) in enumerate(pairs)]
    for copy in copies:
        copy.start()
    for copy in copies:
        copy.wait()


def solution(mesh):
    R, T = mesh.shape["replica"], mesh.shape["tensor"]
    Z = R // 4

    def body(tokens, norm_gain, key_weight, inner_params, outer_params, outer_momentum):
        tr, D = tokens.shape
        nc = key_weight.shape[2]
        rows, FC = inner_params.shape[2:]
        rp = rows // R
        tok = tr * T
        nch = max(1, tr // 64)
        nw = 4
        inner = inner_params.reshape(Z, 2, 2, rp, FC)
        tables = jnp.asarray(rotary_tables(tok))
        sizes = (Z, T, tr, D, nc, rp, FC, nch, nw)
        vm = pltpu.VMEM
        dma = lambda n: pltpu.SemaphoreType.DMA((n,))
        scratch = [
            vm((tr, D), BF16), vm((D,), BF16), vm((D, nc), BF16),
            vm((Z, 2, 2, rp, FC), BF16), vm((1, rp, FC), F32), vm((1, rp, FC), F32),
            vm((2, tok, HD), F32), vm((T, tr, D), BF16), vm((tr, nc), F32), vm((tok, nc), BF16),
            vm((Z, 2, rp, FC), BF16), vm((Z, rp, FC), BF16), vm((Z, rp, FC), F32),
            vm((Z, rp, FC), BF16), vm((Z, rp, FC), BF16), vm((rp, FC), F32),
            vm((Z, rp, FC), BF16), vm((rp, FC), BF16),
            dma(5), dma(nch), dma(nw), dma(3 + T),
            dma(Z), dma(Z), dma(Z), dma(Z), dma(Z), dma(Z),
            dma(Z), dma(Z), dma(Z), dma(Z), dma(Z), dma(Z), dma(Z), dma(Z),
            dma(nch * (T - 1)), dma(nch * (T - 1)),
        ]
        operands = [
            pltpu.with_memory_space_constraint(a, pltpu.HBM)
            for a in (tokens, norm_gain, key_weight, inner, outer_params, outer_momentum, tables)
        ]
        anywhere = pl.BlockSpec(memory_space=pl.ANY)
        keys, outer_next, moment_next, synced = pl.pallas_call(
            functools.partial(kernel, sizes),
            out_shape=(
                vm((tok, nc), BF16),
                vm((1, rp, FC), F32),
                vm((1, rp, FC), F32),
                vm((Z, 2, 2, rp, FC), BF16),
            ),
            in_specs=[anywhere] * 7,
            out_specs=(anywhere,) * 4,
            scratch_shapes=scratch,
            compiler_params=pltpu.CompilerParams(
                collective_id=0, has_side_effects=True, vmem_limit_bytes=VMEM_GRANT
            ),
            name="outer_step_and_keys",
        )(*operands)
        return pl.pallas_call(
            write_out,
            out_shape=(
                jax.ShapeDtypeStruct((tok, nc), BF16),
                jax.ShapeDtypeStruct((1, rp, FC), F32),
                jax.ShapeDtypeStruct((1, rp, FC), F32),
                jax.ShapeDtypeStruct((1, rows, FC), BF16),
            ),
            in_specs=[anywhere] * 4,
            out_specs=(pl.BlockSpec(memory_space=pltpu.HBM),) * 4,
            scratch_shapes=[dma(4)],
            name="write_out",
        )(keys, outer_next, moment_next, synced.reshape(1, rows, FC))

    in_specs = (
        P(("replica", "tensor"), None),
        P(),
        P("replica", None, "tensor"),
        P("replica", "tensor", None, None),
        P("tensor", "replica", None),
        P("tensor", "replica", None),
    )
    out_specs = (
        P("replica", "tensor"),
        P("tensor", "replica", None),
        P("tensor", "replica", None),
        P("tensor", None, None),
    )
    return jax.shard_map(body, mesh=mesh, in_specs=in_specs, out_specs=out_specs, check_vma=False)
```

```python
import functools
import math

import jax
import jax.numpy as jnp
import numpy as np
from jax import lax
from jax.experimental import pallas as pl
from jax.experimental.pallas import tpu as pltpu
from jax.sharding import PartitionSpec as P

HD = 128
EPSILON = 1e-05
ROPE_BASE = 500000.0
LR_OUTER = 0.7
MOMENTUM_OUTER = 0.9

MESH = pl.DeviceIdType.MESH
F32 = jnp.float32
BF16 = jnp.bfloat16

NORM_ROWS = 32
NORM_COLS = 512
K_STEP = 1024
VMEM_GRANT = 48 * 2**20


def rotary_tables(rows):
    half = HD // 2
    index = np.arange(half, dtype=np.float32)
    inverse = np.exp(-(2.0 * index / HD) * math.log(ROPE_BASE)).astype(np.float32)
    angles = (np.arange(rows, dtype=np.float32)[:, None] * inverse[None, :]).astype(np.float64)
    cosine, sine = np.cos(angles), np.sin(angles)
    return np.stack(
        [np.concatenate([cosine, cosine], 1), np.concatenate([-sine, sine], 1)]
    ).astype(np.float32)


def kernel(
    sizes,
    tokens, gain, weight, inner, outer, moment, tables,
    keys_out, outer_out, moment_out, synced,
    tok_v, gain_v, gain_f, w_v, inner_v, outer_v, moment_v, tables_v, normed_v, acc_v, keys_v,
    rs1, part1, keep, rs2, part2, own, rs3, piece_v,
    load_sem, tok_sem, w_sem, store_sem,
    s1_send, s1_recv, s2_send, s2_recv, s3_send, s3_recv,
    gz_send, gz_recv, gx_send, gx_recv, gy_send, gy_recv, diag_send, diag_recv,
    n_send, n_recv,
):
    Z, T, tr, D, nc, rp, FC, nch, nw = sizes
    R = Z * 4
    rep = lax.axis_index("replica")
    me_t = lax.axis_index("tensor")
    z, y, x = rep // 4, lax.rem(rep // 2, 2), lax.rem(rep, 2)
    oy, ox = 1 - y, 1 - x
    x_peer = (z * 4 + y * 2 + ox, me_t)
    y_peer = (z * 4 + oy * 2 + x, me_t)
    offsets = sorted(range(1, Z), key=lambda o: (-min(o, Z - o), o)) + [0]
    last = Z - 1

    def z_at(o):
        return lax.rem(z + o, Z)

    def z_peer(o):
        return (z_at(o) * 4 + y * 2 + x, me_t)

    rows_per = tr // nch
    k_per = D // nw
    load_inner = pltpu.make_async_copy(inner, inner_v, load_sem.at[0])
    load_gain = pltpu.make_async_copy(gain, gain_v, load_sem.at[1])
    load_outer = pltpu.make_async_copy(outer, outer_v, load_sem.at[2])
    load_moment = pltpu.make_async_copy(moment, moment_v, load_sem.at[3])
    load_tables = pltpu.make_async_copy(tables, tables_v, load_sem.at[4])
    load_tok = [
        pltpu.make_async_copy(
            tokens.at[pl.ds(c * rows_per, rows_per)],
            tok_v.at[pl.ds(c * rows_per, rows_per)],
            tok_sem.at[c],
        )
        for c in range(nch)
    ]
    load_w = [
        pltpu.make_async_copy(
            weight.at[0, pl.ds(c * k_per, k_per)], w_v.at[pl.ds(c * k_per, k_per)], w_sem.at[c]
        )
        for c in range(nw)
    ]
    load_inner.start()
    load_gain.start()
    load_tok[0].start()
    for c in range(1, nch):
        load_tok[c].start()
    for c in range(nw):
        load_w[c].start()
    load_outer.start()
    load_moment.start()
    load_tables.start()

    barrier = pltpu.get_barrier_semaphore()
    partners = [x_peer, y_peer]
    partners += [z_peer(o) for o in range(1, Z)]
    partners += [(rep, lax.rem(me_t + k, T)) for k in range(1, T)]
    for partner in partners:
        pl.semaphore_signal(barrier, inc=1, device_id=partner, device_id_type=MESH)
    pl.semaphore_wait(barrier, len(partners))

    sent = []

    def remote(src, dst, send_sem, recv_sem, device):
        return pltpu.make_async_remote_copy(
            src_ref=src, dst_ref=dst, send_sem=send_sem, recv_sem=recv_sem,
            device_id=device, device_id_type=MESH,
        )

    def start(copy):
        copy.start()
        sent.append(copy)
        return copy

    by_x = [o % 2 == 0 for o in offsets]
    first = []
    load_inner.wait()
    for d, o in enumerate(offsets):
        zc = z_at(o)
        src = inner_v.at[zc, :, ox] if by_x[d] else inner_v.at[zc, oy]
        first.append(start(remote(
            src, rs1.at[d], s1_send.at[d], s1_recv.at[d], x_peer if by_x[d] else y_peer)))

    def norm_copy(k, c, source, device):
        rows = pl.ds(c * rows_per, rows_per)
        i = (k - 1) * nch + c
        return remote(
            normed_v.at[source, rows], normed_v.at[source, rows], n_send.at[i], n_recv.at[i], device
        )

    def norm(c):
        if c == 0:
            load_gain.wait()
            for j in range(0, D, NORM_COLS):
                cols = pl.ds(j, NORM_COLS)
                gain_f[:, cols] = gain_v[cols].astype(F32).reshape(1, NORM_COLS)
        load_tok[c].wait()

        def block(i, carry):
            rows = pl.ds(pl.multiple_of(c * rows_per + i * NORM_ROWS, NORM_ROWS), NORM_ROWS)
            total = jnp.zeros((NORM_ROWS, 128), F32)
            for j in range(0, D, 128):
                v = tok_v[rows, pl.ds(j, 128)].astype(F32)
                total = total + v * v
            scale = lax.rsqrt(jnp.sum(total, axis=-1, keepdims=True) / D + EPSILON)
            for j in range(0, D, NORM_COLS):
                cols = pl.ds(j, NORM_COLS)
                v = tok_v[rows, cols].astype(F32)
                normed_v[me_t, rows, cols] = (v * scale * gain_f[:, cols]).astype(BF16)
            return carry

        lax.fori_loop(0, rows_per // NORM_ROWS, block, 0)

    def send_norm(c):
        for k in range(1, T):
            start(norm_copy(k, c, me_t, (rep, lax.rem(me_t + k, T))))

    second, third = [None] * Z, [None] * Z

    def step_a(d):
        zc = z_at(offsets[d])
        first[d].wait_recv()
        if by_x[d]:
            mine, other, to, peer = y, inner_v[zc, oy, x], oy, y_peer
        else:
            mine, other, to, peer = x, inner_v[zc, y, ox], ox, x_peer
        part1[d] = (other.astype(F32) + rs1[d, to].astype(F32)).astype(BF16)
        second[d] = start(remote(part1.at[d], rs2.at[d], s2_send.at[d], s2_recv.at[d], peer))
        keep[d] = inner_v[zc, y, x].astype(F32) + rs1[d, mine].astype(F32)

    def step_b(d):
        second[d].wait_recv()
        total = keep[d] + rs2[d].astype(F32)
        if d == last:
            own[...] = total
        else:
            part2[d] = total.astype(BF16)
            third[d] = start(remote(
                part2.at[d], rs3.at[d], s3_send.at[d], s3_recv.at[d], z_peer(offsets[d])))

    stores = []

    def store(src, dst, i):
        copy = pltpu.make_async_copy(src, dst, store_sem.at[i])
        copy.start()
        stores.append(copy)

    here = synced.at[z, y, x]
    gather_z, gather_x, gather_y, diag = ([None] * Z for _ in range(4))

    def spread(d, src):
        zp = lax.rem(z + Z - offsets[d], Z)
        dst = synced.at[zp, y, x]
        gather_y[d] = start(remote(src, dst, gy_send.at[d], gy_recv.at[d], y_peer))
        gather_x[d] = start(remote(src, dst, gx_send.at[d], gx_recv.at[d], x_peer))

    def step_c():
        load_outer.wait()
        load_moment.wait()
        summed = own[...]
        for d in range(last):
            third[d].wait_recv()
            summed = summed + rs3[d].astype(F32)
        outer_rows = outer_v[0]
        delta = outer_rows - summed / R
        moment_next = MOMENTUM_OUTER * moment_v[0] + delta
        outer_next = outer_rows - LR_OUTER * (delta + MOMENTUM_OUTER * moment_next)
        piece_v[...] = outer_next.astype(BF16)
        for d in range(last):
            gather_z[d] = start(remote(
                piece_v, here, gz_send.at[d], gz_recv.at[d], z_peer(offsets[d])))
        spread(last, piece_v)
        outer_v[0] = outer_next
        moment_v[0] = moment_next
        store(outer_v, outer_out, 0)
        store(moment_v, moment_out, 1)
        store(piece_v, here, 2)

    def step_z(d):
        zp = lax.rem(z + Z - offsets[d], Z)
        gather_z[d].wait_recv()
        spread(d, synced.at[zp, y, x])

    def step_f(d):
        zp = lax.rem(z + Z - offsets[d], Z)
        if by_x[d]:
            gather_y[d].wait_recv()
            piece, peer = synced.at[zp, oy, x], x_peer
        else:
            gather_x[d].wait_recv()
            piece, peer = synced.at[zp, y, ox], y_peer
        diag[d] = start(remote(piece, piece, diag_send.at[d], diag_recv.at[d], peer))

    def project(k, part):
        slot = lax.rem(me_t + T - k, T)
        if k == 0:
            load_w[part].wait()
        elif part == 0:
            for c in range(nch):
                norm_copy(k, c, slot, (rep, lax.rem(me_t + k, T))).wait_recv()

        def block(i, carry):
            depth = pl.ds(pl.multiple_of(part * k_per + i * K_STEP, K_STEP), K_STEP)
            acc_v[...] += jnp.dot(
                normed_v[slot, :, depth], w_v[depth, :], preferred_element_type=F32
            )
            return carry

        if part == 0:
            acc_v[...] = jnp.zeros_like(acc_v)
        lax.fori_loop(0, k_per // K_STEP, block, 0)

    def turn(k):
        slot = lax.rem(me_t + T - k, T)
        if k == 0:
            load_tables.wait()
        rows = pl.ds(pl.multiple_of(slot * tr, tr), tr)
        cosine = tables_v[0, rows]
        sine = tables_v[1, rows]
        for h in range(nc // HD):
            cols = pl.ds(h * HD, HD)
            v = acc_v[:, cols]
            keys_v[rows, cols] = (v * cosine + pltpu.roll(v, HD // 2, 1) * sine).astype(BF16)
        store(keys_v.at[rows], keys_out.at[rows], 3 + k)

    compute = [functools.partial(norm, c) for c in range(nch)]
    for k in range(T):
        compute += [functools.partial(project, k, part) for part in range(nw)]
        compute.append(functools.partial(turn, k))
    compute = compute[::-1]

    def work(count=1):
        for _ in range(count):
            if compute:
                compute.pop()()

    work(1)
    for d in range(Z):
        work(1)
        step_a(d)
        if d >= 1:
            step_b(d - 1)
            if d - 1 < nch:
                send_norm(d - 1)
    step_b(last)
    for c in range(last, nch):
        send_norm(c)
    work(nw + 1 - max(0, Z - nch) - (1 if Z < nch else 0))
    step_c()
    step_f(last)
    for d in range(last):
        step_z(d)
        work(1)
        step_f(d)
        work(1)
    work(len(compute))
    for d in range(Z):
        (gather_x if by_x[d] else gather_y)[d].wait_recv()
        diag[d].wait_recv()
    for copy in sent:
        copy.wait_send()
    for copy in stores:
        copy.wait()


def write_out(keys, outer, moment, synced, keys_out, outer_out, moment_out, synced_out, sem):
    pairs = ((synced, synced_out), (keys, keys_out), (outer, outer_out), (moment, moment_out))
    copies = [pltpu.make_async_copy(a, b, sem.at[i]) for i, (a, b) in enumerate(pairs)]
    for copy in copies:
        copy.start()
    for copy in copies:
        copy.wait()


def solution(mesh):
    R, T = mesh.shape["replica"], mesh.shape["tensor"]
    Z = R // 4

    def body(tokens, norm_gain, key_weight, inner_params, outer_params, outer_momentum):
        tr, D = tokens.shape
        nc = key_weight.shape[2]
        rows, FC = inner_params.shape[2:]
        rp = rows // R
        tok = tr * T
        nch = max(1, tr // 64)
        nw = 4
        inner = inner_params.reshape(Z, 2, 2, rp, FC)
        tables = jnp.asarray(rotary_tables(tok))
        sizes = (Z, T, tr, D, nc, rp, FC, nch, nw)
        vm = pltpu.VMEM
        dma = lambda n: pltpu.SemaphoreType.DMA((n,))
        scratch = [
            vm((tr, D), BF16), vm((D,), BF16), vm((1, D), F32), vm((D, nc), BF16),
            vm((Z, 2, 2, rp, FC), BF16), vm((1, rp, FC), F32), vm((1, rp, FC), F32),
            vm((2, tok, HD), F32), vm((T, tr, D), BF16), vm((tr, nc), F32), vm((tok, nc), BF16),
            vm((Z, 2, rp, FC), BF16), vm((Z, rp, FC), BF16), vm((Z, rp, FC), F32),
            vm((Z, rp, FC), BF16), vm((Z, rp, FC), BF16), vm((rp, FC), F32),
            vm((Z, rp, FC), BF16), vm((rp, FC), BF16),
            dma(5), dma(nch), dma(nw), dma(3 + T),
            dma(Z), dma(Z), dma(Z), dma(Z), dma(Z), dma(Z),
            dma(Z), dma(Z), dma(Z), dma(Z), dma(Z), dma(Z), dma(Z), dma(Z),
            dma(nch * (T - 1)), dma(nch * (T - 1)),
        ]
        operands = [
            pltpu.with_memory_space_constraint(a, pltpu.HBM)
            for a in (tokens, norm_gain, key_weight, inner, outer_params, outer_momentum, tables)
        ]
        anywhere = pl.BlockSpec(memory_space=pl.ANY)
        keys, outer_next, moment_next, synced = pl.pallas_call(
            functools.partial(kernel, sizes),
            out_shape=(
                vm((tok, nc), BF16),
                vm((1, rp, FC), F32),
                vm((1, rp, FC), F32),
                vm((Z, 2, 2, rp, FC), BF16),
            ),
            in_specs=[anywhere] * 7,
            out_specs=(anywhere,) * 4,
            scratch_shapes=scratch,
            compiler_params=pltpu.CompilerParams(
                collective_id=0, has_side_effects=True, vmem_limit_bytes=VMEM_GRANT
            ),
            name="outer_step_and_keys",
        )(*operands)
        results = [
            pltpu.with_memory_space_constraint(a, pltpu.VMEM)
            for a in (keys, outer_next, moment_next, synced.reshape(1, rows, FC))
        ]
        return pl.pallas_call(
            write_out,
            out_shape=(
                jax.ShapeDtypeStruct((tok, nc), BF16),
                jax.ShapeDtypeStruct((1, rp, FC), F32),
                jax.ShapeDtypeStruct((1, rp, FC), F32),
                jax.ShapeDtypeStruct((1, rows, FC), BF16),
            ),
            in_specs=[anywhere] * 4,
            out_specs=(pl.BlockSpec(memory_space=pltpu.HBM),) * 4,
            scratch_shapes=[dma(4)],
            compiler_params=pltpu.CompilerParams(vmem_limit_bytes=16 * 2**20),
            name="write_out",
        )(*results)

    in_specs = (
        P(("replica", "tensor"), None),
        P(),
        P("replica", None, "tensor"),
        P("replica", "tensor", None, None),
        P("tensor", "replica", None),
        P("tensor", "replica", None),
    )
    out_specs = (
        P("replica", "tensor"),
        P("tensor", "replica", None),
        P("tensor", "replica", None),
        P("tensor", None, None),
    )
    return jax.shard_map(body, mesh=mesh, in_specs=in_specs, out_specs=out_specs, check_vma=False)
```

```python
import functools
import math

import jax
import jax.numpy as jnp
import numpy as np
from jax import lax
from jax.experimental import pallas as pl
from jax.experimental.pallas import tpu as pltpu
from jax.sharding import PartitionSpec as P

HD = 128
EPSILON = 1e-05
ROPE_BASE = 500000.0
LR_OUTER = 0.7
MOMENTUM_OUTER = 0.9

MESH = pl.DeviceIdType.MESH
F32 = jnp.float32
BF16 = jnp.bfloat16

NORM_ROWS = 32
NORM_COLS = 512
K_STEP = 1024
VMEM_GRANT = 48 * 2**20


def rotary_tables(rows):
    half = HD // 2
    index = np.arange(half, dtype=np.float32)
    inverse = np.exp(-(2.0 * index / HD) * math.log(ROPE_BASE)).astype(np.float32)
    angles = (np.arange(rows, dtype=np.float32)[:, None] * inverse[None, :]).astype(np.float64)
    cosine, sine = np.cos(angles), np.sin(angles)
    return np.stack(
        [np.concatenate([cosine, cosine], 1), np.concatenate([-sine, sine], 1)]
    ).astype(np.float32)


def kernel(
    sizes,
    tokens, gain, weight, inner, outer, moment, tables,
    keys_out, outer_out, moment_out, synced,
    tok_v, gain_v, gain_f, w_v, inner_v, outer_v, moment_v, tables_v, normed_v, acc_v, keys_v,
    rs1, part1, keep, rs2, part2, own, rs3, piece_v,
    load_sem, tok_sem, w_sem, store_sem,
    s1_send, s1_recv, s2_send, s2_recv, s3_send, s3_recv,
    gz_send, gz_recv, gx_send, gx_recv, gy_send, gy_recv, diag_send, diag_recv,
    n_send, n_recv,
):
    Z, T, tr, D, nc, rp, FC, nch, nw = sizes
    R = Z * 4
    rep = lax.axis_index("replica")
    me_t = lax.axis_index("tensor")
    z, y, x = rep // 4, lax.rem(rep // 2, 2), lax.rem(rep, 2)
    oy, ox = 1 - y, 1 - x
    x_peer = (z * 4 + y * 2 + ox, me_t)
    y_peer = (z * 4 + oy * 2 + x, me_t)
    offsets = sorted(range(1, Z), key=lambda o: (-min(o, Z - o), o)) + [0]
    last = Z - 1

    def z_at(o):
        return lax.rem(z + o, Z)

    def z_peer(o):
        return (z_at(o) * 4 + y * 2 + x, me_t)

    rows_per = tr // nch
    k_per = D // nw
    load_inner = pltpu.make_async_copy(inner, inner_v, load_sem.at[0])
    load_gain = pltpu.make_async_copy(gain, gain_v, load_sem.at[1])
    load_outer = pltpu.make_async_copy(outer, outer_v, load_sem.at[2])
    load_moment = pltpu.make_async_copy(moment, moment_v, load_sem.at[3])
    load_tables = pltpu.make_async_copy(tables, tables_v, load_sem.at[4])
    load_tok = [
        pltpu.make_async_copy(
            tokens.at[pl.ds(c * rows_per, rows_per)],
            tok_v.at[pl.ds(c * rows_per, rows_per)],
            tok_sem.at[c],
        )
        for c in range(nch)
    ]
    load_w = [
        pltpu.make_async_copy(
            weight.at[0, pl.ds(c * k_per, k_per)], w_v.at[pl.ds(c * k_per, k_per)], w_sem.at[c]
        )
        for c in range(nw)
    ]
    load_inner.start()
    load_gain.start()
    load_tok[0].start()
    for c in range(1, nch):
        load_tok[c].start()
    for c in range(nw):
        load_w[c].start()
    load_outer.start()
    load_moment.start()
    load_tables.start()

    barrier = pltpu.get_barrier_semaphore()
    partners = [x_peer, y_peer]
    partners += [z_peer(o) for o in range(1, Z)]
    partners += [(rep, lax.rem(me_t + k, T)) for k in range(1, T)]
    for partner in partners:
        pl.semaphore_signal(barrier, inc=1, device_id=partner, device_id_type=MESH)
    pl.semaphore_wait(barrier, len(partners))

    sent = []

    def remote(src, dst, send_sem, recv_sem, device):
        return pltpu.make_async_remote_copy(
            src_ref=src, dst_ref=dst, send_sem=send_sem, recv_sem=recv_sem,
            device_id=device, device_id_type=MESH,
        )

    def start(copy):
        copy.start()
        sent.append(copy)
        return copy

    by_x = [o % 2 == 0 for o in offsets]
    first = []
    load_inner.wait()
    for d, o in enumerate(offsets):
        zc = z_at(o)
        src = inner_v.at[zc, :, ox] if by_x[d] else inner_v.at[zc, oy]
        first.append(start(remote(
            src, rs1.at[d], s1_send.at[d], s1_recv.at[d], x_peer if by_x[d] else y_peer)))

    def norm_copy(k, c, source, device):
        rows = pl.ds(c * rows_per, rows_per)
        i = (k - 1) * nch + c
        return remote(
            normed_v.at[source, rows], normed_v.at[source, rows], n_send.at[i], n_recv.at[i], device
        )

    def norm(c):
        if c == 0:
            load_gain.wait()
            for j in range(0, D, NORM_COLS):
                cols = pl.ds(j, NORM_COLS)
                gain_f[:, cols] = gain_v[cols].astype(F32).reshape(1, NORM_COLS)
        load_tok[c].wait()

        def block(i, carry):
            rows = pl.ds(pl.multiple_of(c * rows_per + i * NORM_ROWS, NORM_ROWS), NORM_ROWS)
            total = jnp.zeros((NORM_ROWS, 128), F32)
            for j in range(0, D, 128):
                v = tok_v[rows, pl.ds(j, 128)].astype(F32)
                total = total + v * v
            scale = lax.rsqrt(jnp.sum(total, axis=-1, keepdims=True) / D + EPSILON)
            for j in range(0, D, NORM_COLS):
                cols = pl.ds(j, NORM_COLS)
                v = tok_v[rows, cols].astype(F32)
                normed_v[me_t, rows, cols] = (v * scale * gain_f[:, cols]).astype(BF16)
            return carry

        lax.fori_loop(0, rows_per // NORM_ROWS, block, 0)
        for k in range(1, T):
            start(norm_copy(k, c, me_t, (rep, lax.rem(me_t + k, T))))

    second, third = [None] * Z, [None] * Z

    def step_a(d):
        zc = z_at(offsets[d])
        first[d].wait_recv()
        if by_x[d]:
            mine, other, to, peer = y, inner_v[zc, oy, x], oy, y_peer
        else:
            mine, other, to, peer = x, inner_v[zc, y, ox], ox, x_peer
        part1[d] = (other.astype(F32) + rs1[d, to].astype(F32)).astype(BF16)
        second[d] = start(remote(part1.at[d], rs2.at[d], s2_send.at[d], s2_recv.at[d], peer))
        keep[d] = inner_v[zc, y, x].astype(F32) + rs1[d, mine].astype(F32)

    def step_b(d):
        second[d].wait_recv()
        total = keep[d] + rs2[d].astype(F32)
        if d == last:
            own[...] = total
        else:
            part2[d] = total.astype(BF16)
            third[d] = start(remote(
                part2.at[d], rs3.at[d], s3_send.at[d], s3_recv.at[d], z_peer(offsets[d])))

    stores = []

    def store(src, dst, i):
        copy = pltpu.make_async_copy(src, dst, store_sem.at[i])
        copy.start()
        stores.append(copy)

    here = synced.at[z, y, x]
    gather_z, gather_x, gather_y, diag = ([None] * Z for _ in range(4))

    def spread(d, src):
        zp = lax.rem(z + Z - offsets[d], Z)
        dst = synced.at[zp, y, x]
        gather_y[d] = start(remote(src, dst, gy_send.at[d], gy_recv.at[d], y_peer))
        gather_x[d] = start(remote(src, dst, gx_send.at[d], gx_recv.at[d], x_peer))

    def step_c():
        load_outer.wait()
        load_moment.wait()
        summed = own[...]
        for d in range(last):
            third[d].wait_recv()
            summed = summed + rs3[d].astype(F32)
        outer_rows = outer_v[0]
        delta = outer_rows - summed / R
        moment_next = MOMENTUM_OUTER * moment_v[0] + delta
        outer_next = outer_rows - LR_OUTER * (delta + MOMENTUM_OUTER * moment_next)
        piece_v[...] = outer_next.astype(BF16)
        for d in range(last):
            gather_z[d] = start(remote(
                piece_v, here, gz_send.at[d], gz_recv.at[d], z_peer(offsets[d])))
        spread(last, piece_v)
        outer_v[0] = outer_next
        moment_v[0] = moment_next
        store(outer_v, outer_out, 0)
        store(moment_v, moment_out, 1)
        store(piece_v, here, 2)

    def step_z(d):
        zp = lax.rem(z + Z - offsets[d], Z)
        gather_z[d].wait_recv()
        spread(d, synced.at[zp, y, x])

    def step_f(d):
        zp = lax.rem(z + Z - offsets[d], Z)
        if by_x[d]:
            gather_y[d].wait_recv()
            piece, peer = synced.at[zp, oy, x], x_peer
        else:
            gather_x[d].wait_recv()
            piece, peer = synced.at[zp, y, ox], y_peer
        diag[d] = start(remote(piece, piece, diag_send.at[d], diag_recv.at[d], peer))

    def project(k, part):
        slot = lax.rem(me_t + T - k, T)
        if k == 0:
            load_w[part].wait()
        elif part == 0:
            for c in range(nch):
                norm_copy(k, c, slot, (rep, lax.rem(me_t + k, T))).wait_recv()

        def block(i, carry):
            depth = pl.ds(pl.multiple_of(part * k_per + i * K_STEP, K_STEP), K_STEP)
            acc_v[...] += jnp.dot(
                normed_v[slot, :, depth], w_v[depth, :], preferred_element_type=F32
            )
            return carry

        if part == 0:
            acc_v[...] = jnp.zeros_like(acc_v)
        lax.fori_loop(0, k_per // K_STEP, block, 0)

    def turn(k):
        slot = lax.rem(me_t + T - k, T)
        if k == 0:
            load_tables.wait()
        rows = pl.ds(pl.multiple_of(slot * tr, tr), tr)
        cosine = tables_v[0, rows]
        sine = tables_v[1, rows]
        for h in range(nc // HD):
            cols = pl.ds(h * HD, HD)
            v = acc_v[:, cols]
            keys_v[rows, cols] = (v * cosine + pltpu.roll(v, HD // 2, 1) * sine).astype(BF16)
        store(keys_v.at[rows], keys_out.at[rows], 3 + k)

    compute = [functools.partial(norm, c) for c in range(nch)]
    for k in range(T):
        compute += [functools.partial(project, k, part) for part in range(nw)]
        compute.append(functools.partial(turn, k))
    compute = compute[::-1]

    def work(count=1):
        for _ in range(count):
            if compute:
                compute.pop()()

    work(1)
    for d in range(Z):
        work(1)
        step_a(d)
        if d >= 1:
            step_b(d - 1)
    step_b(last)
    work(len(compute) - (T - 1) * (nw + 1))
    step_c()
    step_f(last)
    for d in range(last):
        step_z(d)
        step_f(d)
        if d == last - 2:
            work(2)
    work(len(compute))
    for d in range(Z):
        (gather_x if by_x[d] else gather_y)[d].wait_recv()
        diag[d].wait_recv()
    for copy in sent:
        copy.wait_send()
    for copy in stores:
        copy.wait()


def write_out(keys, outer, moment, synced, keys_out, outer_out, moment_out, synced_out, sem):
    pairs = ((synced, synced_out), (keys, keys_out), (outer, outer_out), (moment, moment_out))
    copies = [pltpu.make_async_copy(a, b, sem.at[i]) for i, (a, b) in enumerate(pairs)]
    for copy in copies:
        copy.start()
    for copy in copies:
        copy.wait()


def solution(mesh):
    R, T = mesh.shape["replica"], mesh.shape["tensor"]
    Z = R // 4

    def body(tokens, norm_gain, key_weight, inner_params, outer_params, outer_momentum):
        tr, D = tokens.shape
        nc = key_weight.shape[2]
        rows, FC = inner_params.shape[2:]
        rp = rows // R
        tok = tr * T
        nch = max(1, tr // 64)
        nw = 4
        inner = inner_params.reshape(Z, 2, 2, rp, FC)
        tables = jnp.asarray(rotary_tables(tok))
        sizes = (Z, T, tr, D, nc, rp, FC, nch, nw)
        vm = pltpu.VMEM
        dma = lambda n: pltpu.SemaphoreType.DMA((n,))
        scratch = [
            vm((tr, D), BF16), vm((D,), BF16), vm((1, D), F32), vm((D, nc), BF16),
            vm((Z, 2, 2, rp, FC), BF16), vm((1, rp, FC), F32), vm((1, rp, FC), F32),
            vm((2, tok, HD), F32), vm((T, tr, D), BF16), vm((tr, nc), F32), vm((tok, nc), BF16),
            vm((Z, 2, rp, FC), BF16), vm((Z, rp, FC), BF16), vm((Z, rp, FC), F32),
            vm((Z, rp, FC), BF16), vm((Z, rp, FC), BF16), vm((rp, FC), F32),
            vm((Z, rp, FC), BF16), vm((rp, FC), BF16),
            dma(5), dma(nch), dma(nw), dma(3 + T),
            dma(Z), dma(Z), dma(Z), dma(Z), dma(Z), dma(Z),
            dma(Z), dma(Z), dma(Z), dma(Z), dma(Z), dma(Z), dma(Z), dma(Z),
            dma(nch * (T - 1)), dma(nch * (T - 1)),
        ]
        operands = [
            pltpu.with_memory_space_constraint(a, pltpu.HBM)
            for a in (tokens, norm_gain, key_weight, inner, outer_params, outer_momentum, tables)
        ]
        anywhere = pl.BlockSpec(memory_space=pl.ANY)
        keys, outer_next, moment_next, synced = pl.pallas_call(
            functools.partial(kernel, sizes),
            out_shape=(
                vm((tok, nc), BF16),
                vm((1, rp, FC), F32),
                vm((1, rp, FC), F32),
                vm((Z, 2, 2, rp, FC), BF16),
            ),
            in_specs=[anywhere] * 7,
            out_specs=(anywhere,) * 4,
            scratch_shapes=scratch,
            compiler_params=pltpu.CompilerParams(
                collective_id=0, has_side_effects=True, vmem_limit_bytes=VMEM_GRANT
            ),
            name="outer_step_and_keys",
        )(*operands)
        results = [
            pltpu.with_memory_space_constraint(a, pltpu.VMEM)
            for a in (keys, outer_next, moment_next, synced.reshape(1, rows, FC))
        ]
        return pl.pallas_call(
            write_out,
            out_shape=(
                jax.ShapeDtypeStruct((tok, nc), BF16),
                jax.ShapeDtypeStruct((1, rp, FC), F32),
                jax.ShapeDtypeStruct((1, rp, FC), F32),
                jax.ShapeDtypeStruct((1, rows, FC), BF16),
            ),
            in_specs=[anywhere] * 4,
            out_specs=(pl.BlockSpec(memory_space=pltpu.HBM),) * 4,
            scratch_shapes=[dma(4)],
            compiler_params=pltpu.CompilerParams(vmem_limit_bytes=16 * 2**20),
            name="write_out",
        )(*results)

    in_specs = (
        P(("replica", "tensor"), None),
        P(),
        P("replica", None, "tensor"),
        P("replica", "tensor", None, None),
        P("tensor", "replica", None),
        P("tensor", "replica", None),
    )
    out_specs = (
        P("replica", "tensor"),
        P("tensor", "replica", None),
        P("tensor", "replica", None),
        P("tensor", None, None),
    )
    return jax.shard_map(body, mesh=mesh, in_specs=in_specs, out_specs=out_specs, check_vma=False)
```

```python
import functools
import math

import jax
import jax.numpy as jnp
import numpy as np
from jax import lax
from jax.experimental import pallas as pl
from jax.experimental.pallas import tpu as pltpu
from jax.sharding import PartitionSpec as P

HD = 128
EPSILON = 1e-05
ROPE_BASE = 500000.0
LR_OUTER = 0.7
MOMENTUM_OUTER = 0.9

MESH = pl.DeviceIdType.MESH
F32 = jnp.float32
BF16 = jnp.bfloat16

NORM_ROWS = 32
NORM_COLS = 512
K_STEP = 1024
VMEM_GRANT = 48 * 2**20


def rotary_tables(rows):
    half = HD // 2
    index = np.arange(half, dtype=np.float32)
    inverse = np.exp(-(2.0 * index / HD) * math.log(ROPE_BASE)).astype(np.float32)
    angles = (np.arange(rows, dtype=np.float32)[:, None] * inverse[None, :]).astype(np.float64)
    cosine, sine = np.cos(angles), np.sin(angles)
    return np.stack(
        [np.concatenate([cosine, cosine], 1), np.concatenate([-sine, sine], 1)]
    ).astype(np.float32)


def kernel(
    sizes,
    tokens, gain, weight, inner, outer, moment, tables,
    keys_out, outer_out, moment_out, synced,
    tok_v, gain_v, gain_f, w_v, inner_v, outer_v, moment_v, tables_v, normed_v, acc_v, keys_v,
    rs1, part1, keep, rs2, part2, own, rs3, piece_v,
    load_sem, tok_sem, w_sem, store_sem,
    s1_send, s1_recv, s2_send, s2_recv, s3_send, s3_recv,
    gz_send, gz_recv, gx_send, gx_recv, gy_send, gy_recv, diag_send, diag_recv,
    n_send, n_recv,
):
    Z, T, tr, D, nc, rp, FC, nch, nw = sizes
    R = Z * 4
    rep = lax.axis_index("replica")
    me_t = lax.axis_index("tensor")
    z, y, x = rep // 4, lax.rem(rep // 2, 2), lax.rem(rep, 2)
    oy, ox = 1 - y, 1 - x
    x_peer = (z * 4 + y * 2 + ox, me_t)
    y_peer = (z * 4 + oy * 2 + x, me_t)
    offsets = sorted(range(1, Z), key=lambda o: (-min(o, Z - o), o)) + [0]
    last = Z - 1

    def z_at(o):
        return lax.rem(z + o, Z)

    def z_peer(o):
        return (z_at(o) * 4 + y * 2 + x, me_t)

    rows_per = tr // nch
    k_per = D // nw
    load_inner = pltpu.make_async_copy(inner, inner_v, load_sem.at[0])
    load_gain = pltpu.make_async_copy(gain, gain_v, load_sem.at[1])
    load_outer = pltpu.make_async_copy(outer, outer_v, load_sem.at[2])
    load_moment = pltpu.make_async_copy(moment, moment_v, load_sem.at[3])
    load_tables = pltpu.make_async_copy(tables, tables_v, load_sem.at[4])
    load_tok = [
        pltpu.make_async_copy(
            tokens.at[pl.ds(c * rows_per, rows_per)],
            tok_v.at[pl.ds(c * rows_per, rows_per)],
            tok_sem.at[c],
        )
        for c in range(nch)
    ]
    load_w = [
        pltpu.make_async_copy(
            weight.at[0, pl.ds(c * k_per, k_per)], w_v.at[pl.ds(c * k_per, k_per)], w_sem.at[c]
        )
        for c in range(nw)
    ]
    load_inner.start()
    load_gain.start()
    load_tok[0].start()
    for c in range(1, nch):
        load_tok[c].start()
    for c in range(nw):
        load_w[c].start()
    load_outer.start()
    load_moment.start()
    load_tables.start()

    barrier = pltpu.get_barrier_semaphore()
    partners = [x_peer, y_peer]
    partners += [z_peer(o) for o in range(1, Z)]
    partners += [(rep, lax.rem(me_t + k, T)) for k in range(1, T)]
    for partner in partners:
        pl.semaphore_signal(barrier, inc=1, device_id=partner, device_id_type=MESH)
    pl.semaphore_wait(barrier, len(partners))

    sent = []

    def remote(src, dst, send_sem, recv_sem, device):
        return pltpu.make_async_remote_copy(
            src_ref=src, dst_ref=dst, send_sem=send_sem, recv_sem=recv_sem,
            device_id=device, device_id_type=MESH,
        )

    def start(copy):
        copy.start()
        sent.append(copy)
        return copy

    by_x = [o % 2 == 0 for o in offsets]
    first = []
    load_inner.wait()
    for d, o in enumerate(offsets):
        zc = z_at(o)
        src = inner_v.at[zc, :, ox] if by_x[d] else inner_v.at[zc, oy]
        first.append(start(remote(
            src, rs1.at[d], s1_send.at[d], s1_recv.at[d], x_peer if by_x[d] else y_peer)))

    def norm_copy(k, c, source, device):
        rows = pl.ds(c * rows_per, rows_per)
        i = (k - 1) * nch + c
        return remote(
            normed_v.at[source, rows], normed_v.at[source, rows], n_send.at[i], n_recv.at[i], device
        )

    def norm(c):
        if c == 0:
            load_gain.wait()
            for j in range(0, D, NORM_COLS):
                cols = pl.ds(j, NORM_COLS)
                gain_f[:, cols] = gain_v[cols].astype(F32).reshape(1, NORM_COLS)
        load_tok[c].wait()

        def block(i, carry):
            rows = pl.ds(pl.multiple_of(c * rows_per + i * NORM_ROWS, NORM_ROWS), NORM_ROWS)
            total = jnp.zeros((NORM_ROWS, 128), F32)
            for j in range(0, D, 128):
                v = tok_v[rows, pl.ds(j, 128)].astype(F32)
                total = total + v * v
            scale = lax.rsqrt(jnp.sum(total, axis=-1, keepdims=True) / D + EPSILON)
            for j in range(0, D, NORM_COLS):
                cols = pl.ds(j, NORM_COLS)
                v = tok_v[rows, cols].astype(F32)
                normed_v[me_t, rows, cols] = (v * scale * gain_f[:, cols]).astype(BF16)
            return carry

        lax.fori_loop(0, rows_per // NORM_ROWS, block, 0)
        for k in range(1, T):
            start(norm_copy(k, c, me_t, (rep, lax.rem(me_t + k, T))))

    second, third = [None] * Z, [None] * Z

    def step_a(d):
        zc = z_at(offsets[d])
        first[d].wait_recv()
        if by_x[d]:
            mine, other, to, peer = y, inner_v[zc, oy, x], oy, y_peer
        else:
            mine, other, to, peer = x, inner_v[zc, y, ox], ox, x_peer
        part1[d] = (other.astype(F32) + rs1[d, to].astype(F32)).astype(BF16)
        second[d] = start(remote(part1.at[d], rs2.at[d], s2_send.at[d], s2_recv.at[d], peer))
        keep[d] = inner_v[zc, y, x].astype(F32) + rs1[d, mine].astype(F32)

    def step_b(d):
        second[d].wait_recv()
        total = keep[d] + rs2[d].astype(F32)
        if d == last:
            own[...] = total
        else:
            part2[d] = total.astype(BF16)
            third[d] = start(remote(
                part2.at[d], rs3.at[d], s3_send.at[d], s3_recv.at[d], z_peer(offsets[d])))

    stores = []

    def store(src, dst, i):
        copy = pltpu.make_async_copy(src, dst, store_sem.at[i])
        copy.start()
        stores.append(copy)

    here = synced.at[z, y, x]
    gather_z, gather_x, gather_y, diag = ([None] * Z for _ in range(4))

    def spread(d, src):
        zp = lax.rem(z + Z - offsets[d], Z)
        dst = synced.at[zp, y, x]
        gather_y[d] = start(remote(src, dst, gy_send.at[d], gy_recv.at[d], y_peer))
        gather_x[d] = start(remote(src, dst, gx_send.at[d], gx_recv.at[d], x_peer))

    def step_c():
        load_outer.wait()
        load_moment.wait()
        summed = own[...]
        for d in range(last):
            third[d].wait_recv()
            summed = summed + rs3[d].astype(F32)
        outer_rows = outer_v[0]
        delta = outer_rows - summed / R
        moment_next = MOMENTUM_OUTER * moment_v[0] + delta
        outer_next = outer_rows - LR_OUTER * (delta + MOMENTUM_OUTER * moment_next)
        piece_v[...] = outer_next.astype(BF16)
        for d in range(last):
            gather_z[d] = start(remote(
                piece_v, here, gz_send.at[d], gz_recv.at[d], z_peer(offsets[d])))
        spread(last, piece_v)
        outer_v[0] = outer_next
        moment_v[0] = moment_next
        store(outer_v, outer_out, 0)
        store(moment_v, moment_out, 1)
        store(piece_v, here, 2)

    def step_z(d):
        zp = lax.rem(z + Z - offsets[d], Z)
        gather_z[d].wait_recv()
        spread(d, synced.at[zp, y, x])

    def step_f(d):
        zp = lax.rem(z + Z - offsets[d], Z)
        if by_x[d]:
            gather_y[d].wait_recv()
            piece, peer = synced.at[zp, oy, x], x_peer
        else:
            gather_x[d].wait_recv()
            piece, peer = synced.at[zp, y, ox], y_peer
        diag[d] = start(remote(piece, piece, diag_send.at[d], diag_recv.at[d], peer))

    def project(k, part):
        slot = lax.rem(me_t + T - k, T)
        if k == 0:
            load_w[part].wait()
        elif part == 0:
            for c in range(nch):
                norm_copy(k, c, slot, (rep, lax.rem(me_t + k, T))).wait_recv()

        def block(i, carry):
            depth = pl.ds(pl.multiple_of(part * k_per + i * K_STEP, K_STEP), K_STEP)
            acc_v[...] += jnp.dot(
                normed_v[slot, :, depth], w_v[depth, :], preferred_element_type=F32
            )
            return carry

        if part == 0:
            acc_v[...] = jnp.zeros_like(acc_v)
        lax.fori_loop(0, k_per // K_STEP, block, 0)

    def turn(k):
        slot = lax.rem(me_t + T - k, T)
        if k == 0:
            load_tables.wait()
        rows = pl.ds(pl.multiple_of(slot * tr, tr), tr)
        cosine = tables_v[0, rows]
        sine = tables_v[1, rows]
        for h in range(nc // HD):
            cols = pl.ds(h * HD, HD)
            v = acc_v[:, cols]
            keys_v[rows, cols] = (v * cosine + pltpu.roll(v, HD // 2, 1) * sine).astype(BF16)
        store(keys_v.at[rows], keys_out.at[rows], 3 + k)

    compute = [functools.partial(norm, c) for c in range(nch)]
    for k in range(T):
        compute += [functools.partial(project, k, part) for part in range(nw)]
        compute.append(functools.partial(turn, k))
    compute = compute[::-1]

    def work(count=1):
        for _ in range(count):
            if compute:
                compute.pop()()

    work(nch)
    for d in range(Z):
        work(1)
        step_a(d)
        if d >= 1:
            step_b(d - 1)
    step_b(last)
    work(len(compute) - (T - 1) * (nw + 1))
    step_c()
    step_f(last)
    for d in range(last):
        step_z(d)
        step_f(d)
        if d == last - 2:
            work(2)
    work(len(compute))
    for d in range(Z):
        (gather_x if by_x[d] else gather_y)[d].wait_recv()
        diag[d].wait_recv()
    for copy in sent:
        copy.wait_send()
    for copy in stores:
        copy.wait()


def write_out(keys, outer, moment, synced, keys_out, outer_out, moment_out, synced_out, sem):
    pairs = ((synced, synced_out), (keys, keys_out), (outer, outer_out), (moment, moment_out))
    copies = [pltpu.make_async_copy(a, b, sem.at[i]) for i, (a, b) in enumerate(pairs)]
    for copy in copies:
        copy.start()
    for copy in copies:
        copy.wait()


def solution(mesh):
    R, T = mesh.shape["replica"], mesh.shape["tensor"]
    Z = R // 4

    def body(tokens, norm_gain, key_weight, inner_params, outer_params, outer_momentum):
        tr, D = tokens.shape
        nc = key_weight.shape[2]
        rows, FC = inner_params.shape[2:]
        rp = rows // R
        tok = tr * T
        nch = max(1, tr // 64)
        nw = 4
        inner = inner_params.reshape(Z, 2, 2, rp, FC)
        tables = jnp.asarray(rotary_tables(tok))
        sizes = (Z, T, tr, D, nc, rp, FC, nch, nw)
        vm = pltpu.VMEM
        dma = lambda n: pltpu.SemaphoreType.DMA((n,))
        scratch = [
            vm((tr, D), BF16), vm((D,), BF16), vm((1, D), F32), vm((D, nc), BF16),
            vm((Z, 2, 2, rp, FC), BF16), vm((1, rp, FC), F32), vm((1, rp, FC), F32),
            vm((2, tok, HD), F32), vm((T, tr, D), BF16), vm((tr, nc), F32), vm((tok, nc), BF16),
            vm((Z, 2, rp, FC), BF16), vm((Z, rp, FC), BF16), vm((Z, rp, FC), F32),
            vm((Z, rp, FC), BF16), vm((Z, rp, FC), BF16), vm((rp, FC), F32),
            vm((Z, rp, FC), BF16), vm((rp, FC), BF16),
            dma(5), dma(nch), dma(nw), dma(3 + T),
            dma(Z), dma(Z), dma(Z), dma(Z), dma(Z), dma(Z),
            dma(Z), dma(Z), dma(Z), dma(Z), dma(Z), dma(Z), dma(Z), dma(Z),
            dma(nch * (T - 1)), dma(nch * (T - 1)),
        ]
        operands = [
            pltpu.with_memory_space_constraint(a, pltpu.HBM)
            for a in (tokens, norm_gain, key_weight, inner, outer_params, outer_momentum, tables)
        ]
        anywhere = pl.BlockSpec(memory_space=pl.ANY)
        keys, outer_next, moment_next, synced = pl.pallas_call(
            functools.partial(kernel, sizes),
            out_shape=(
                vm((tok, nc), BF16),
                vm((1, rp, FC), F32),
                vm((1, rp, FC), F32),
                vm((Z, 2, 2, rp, FC), BF16),
            ),
            in_specs=[anywhere] * 7,
            out_specs=(anywhere,) * 4,
            scratch_shapes=scratch,
            compiler_params=pltpu.CompilerParams(
                collective_id=0, has_side_effects=True, vmem_limit_bytes=VMEM_GRANT
            ),
            name="outer_step_and_keys",
        )(*operands)
        results = [
            pltpu.with_memory_space_constraint(a, pltpu.VMEM)
            for a in (keys, outer_next, moment_next, synced.reshape(1, rows, FC))
        ]
        return pl.pallas_call(
            write_out,
            out_shape=(
                jax.ShapeDtypeStruct((tok, nc), BF16),
                jax.ShapeDtypeStruct((1, rp, FC), F32),
                jax.ShapeDtypeStruct((1, rp, FC), F32),
                jax.ShapeDtypeStruct((1, rows, FC), BF16),
            ),
            in_specs=[anywhere] * 4,
            out_specs=(pl.BlockSpec(memory_space=pltpu.HBM),) * 4,
            scratch_shapes=[dma(4)],
            compiler_params=pltpu.CompilerParams(vmem_limit_bytes=16 * 2**20),
            name="write_out",
        )(*results)

    in_specs = (
        P(("replica", "tensor"), None),
        P(),
        P("replica", None, "tensor"),
        P("replica", "tensor", None, None),
        P("tensor", "replica", None),
        P("tensor", "replica", None),
    )
    out_specs = (
        P("replica", "tensor"),
        P("tensor", "replica", None),
        P("tensor", "replica", None),
        P("tensor", None, None),
    )
    return jax.shard_map(body, mesh=mesh, in_specs=in_specs, out_specs=out_specs, check_vma=False)
```
